32 devices in a mesh: cfg: 2 (over y), tm: 8 (over z, x), space: 2 (over core).
Axes of the slice: x: 2, y: 2, z: 4, core: 2. Of those that a mesh axis runs over, the one named last changes fastest.
Arguments:
- vectors: bfloat16 [16, 2, 3, 8, 4, 16, 128], P(('cfg', 'tm'), None, None, 'space'), parts along dimension 0, may hold values from -6 to 6
- gauge_links: float32 [16, 3, 2, 3, 3, 8, 4, 16], P(('cfg', 'tm'), None, None, None, None, 'space'), parts along dimension 0, may hold values from -2.5 to 2.5
- perambulators: bfloat16 [16, 8, 4, 128, 256], P(('cfg', 'tm')), parts along dimension 0, may hold values from -0.375 to 0.375
- momenta: int32 [8, 3], replicated, may hold values from -2 to 2
- displacements: int32 [8], replicated, may hold values from 0 to 3, as said below
Outputs:
- elementals: bfloat16 [16, 8, 128, 256], P(('cfg', 'tm'), None, 'space'), parts along dimension 0
- correlators: float32 [8, 16, 8], P(None, ('cfg', 'tm')), parts along dimension 1
The draws below stay inside these ranges and needn't reach their ends.
There are 2 independent parts, one for each index of `cfg`. The reference program is written for one: setup_inputs(seed, part) draws one part's arguments, and reference() takes and returns one part's arrays. A program takes and returns all parts, laid end to end along the dimension named above; an argument that names none is the same for every part. Nothing has to cross between parts.
Inputs may be any that keep to these rules, and one draw needn't show every extreme that they name: `displacements`: each of the values 0, 1, 2, 3 appears exactly 2 times.
All inputs are finite; a program needn't handle non-finite values.
Results may differ from the reference program's by a relative error of at most 0.0075.
Values may be sent and summed in bfloat16 or wider, within the bound.
A program may use at most 64 MiB of HBM per device.

```python
import math
import jax
import jax.numpy as jnp
from jax import lax

EIGEN_COUNT = 128
NSPIN = 4
NOP = 8
NDELTA = 8
LY = 4
LZ = 16
NT = 8
LX = 8
SITES = 512


def draw_displacements(key, part):
    pattern = jnp.arange(NOP, dtype=jnp.int32) % 4
    return jax.random.permutation(key, pattern)


def set_ends(entries, stream_key, low, largest):
    longest = entries.shape.index(max(entries.shape))
    spots = []
    for shift in (0, 1):
        where = [jax.random.randint(jax.random.fold_in(stream_key, axis), (), 0, length) for axis, length in enumerate(entries.shape)]
        where[longest] = (where[longest] + shift) % entries.shape[longest]
        spots.append(tuple(where))
    return entries.at[spots[0]].set(low).at[spots[1]].set(largest)


def levels(own_key, shape, shards, low, top_value):
    def one(axis_at, blocks):
        heights = jax.random.uniform(jax.random.fold_in(jax.random.fold_in(own_key, 6), axis_at), (blocks,), jnp.float32, low / len(shards), top_value / len(shards))
        return jnp.repeat(jnp.exp(heights), shape[axis_at] // blocks).reshape((-1,) + (1,) * (len(shape) - axis_at - 1))

    level = one(*shards[0])
    for cut in shards[1:]:
        level = level * one(*cut)
    return level


def gaussian(stream_key, shape, width, limit, cuts=(), held_as=jnp.bfloat16):
    result = jax.random.normal(stream_key, shape, jnp.float32) * width
    if len(cuts) > 0:
        result = levels(stream_key, shape, cuts, -0.22, 0.18) * result
    return jnp.clip(result, min=-limit, max=limit).astype(held_as)


def setup_inputs(seed: int = 0, part: int = 0) -> dict:
    arg_keys = jax.random.split(jax.random.key(seed), 6)
    part_keys = jax.random.split(jax.random.fold_in(arg_keys[5], part), 6)
    vectors = gaussian(part_keys[0], (NT, 2, 3, LX, LY, LZ, EIGEN_COUNT), 1.0, 6.0, ((0, 8), (3, 2)))
    gauge_links = gaussian(part_keys[1], (NT, 3, 2, 3, 3, LX, LY, LZ), 6 ** -0.5, 2.5, ((0, 8), (5, 2)), jnp.float32)
    perambulators = gaussian(part_keys[2], (NT, NDELTA, NSPIN, EIGEN_COUNT, 2 * EIGEN_COUNT), (2 * EIGEN_COUNT) ** -0.5, 0.375, ((0, 8),))
    momenta = set_ends(jax.random.randint(arg_keys[3], (NOP, 3), -2, 3), jax.random.fold_in(arg_keys[3], 1), -2, 2).astype(jnp.int32)
    displacements = draw_displacements(jax.random.fold_in(arg_keys[5], 71), part)
    return dict(vectors=vectors, gauge_links=gauge_links, perambulators=perambulators, momenta=momenta, displacements=displacements)


def link_times(link_matrix, vector_field):
    real_rows = []
    imag_rows = []
    for target in range(3):
        real_sum = jnp.zeros_like(vector_field[0, 0])
        imag_sum = jnp.zeros_like(vector_field[0, 0])
        for source in range(3):
            entry_real = link_matrix[0, target, source][..., None]
            entry_imag = link_matrix[1, target, source][..., None]
            real_sum = real_sum + entry_real * vector_field[0, source] - entry_imag * vector_field[1, source]
            imag_sum = imag_sum + entry_real * vector_field[1, source] + entry_imag * vector_field[0, source]
        real_rows.append(real_sum)
        imag_rows.append(imag_sum)
    return jnp.stack([jnp.stack(real_rows), jnp.stack(imag_rows)])

def adjoint(link_matrix):
    return jnp.stack([jnp.swapaxes(link_matrix[0], 0, 1), -jnp.swapaxes(link_matrix[1], 0, 1)])

def smeared_fields(vector_slice, link_slice):
    vector_field = vector_slice.astype(jnp.float32)
    neighbour_sum = jnp.zeros_like(vector_field)
    displaced = []
    for direction in range(3):
        spatial_axis = 2 + direction
        link_matrix = link_slice[direction]
        forward = link_times(link_matrix, jnp.roll(vector_field, -1, spatial_axis))
        backward = jnp.roll(link_times(adjoint(link_matrix), vector_field), 1, spatial_axis)
        neighbour_sum = neighbour_sum + forward + backward
        displaced.append(forward.astype(jnp.bfloat16))
    smoothed = (vector_field - neighbour_sum / 6.0).astype(jnp.bfloat16)
    return jnp.stack([smoothed] + displaced)

def phased(vector_slice, momentum, x_position, extent_x):
    extent_y = vector_slice.shape[3]
    extent_z = vector_slice.shape[4]
    y_position = jnp.arange(extent_y, dtype=jnp.int32).astype(jnp.float32)
    z_position = jnp.arange(extent_z, dtype=jnp.int32).astype(jnp.float32)
    momentum_float = momentum.astype(jnp.float32)
    phase_angle = (momentum_float[0] * x_position / extent_x)[:, None, None]
    phase_angle = phase_angle + (momentum_float[1] * y_position / extent_y)[None, :, None]
    phase_angle = phase_angle + (momentum_float[2] * z_position / extent_z)[None, None, :]
    phase_angle = 2.0 * math.pi * phase_angle
    cosine = jnp.cos(phase_angle)[..., None]
    sine_part = jnp.sin(phase_angle)[..., None]
    vector_field = vector_slice.astype(jnp.float32)
    left_real = vector_field[0] * cosine - vector_field[1] * sine_part
    left_imag = vector_field[0] * sine_part + vector_field[1] * cosine
    return jnp.stack([left_real, left_imag]).astype(jnp.bfloat16)

def project(left_field, right_field):
    column_entries = left_field.shape[-1]
    left_flat = left_field.reshape(-1, column_entries)
    rotated = jnp.stack([right_field[1], -right_field[0]])
    right_flat = jnp.concatenate([right_field.reshape(-1, column_entries), rotated.reshape(-1, column_entries)], axis=1)
    return jnp.dot(left_flat.T, right_flat, preferred_element_type=jnp.float32)

def operator_terms(fields, vector_slice, momenta, displacements, x_position, extent_x):
    partial_value = []
    for operator in range(momenta.shape[0]):
        left_field = phased(vector_slice, momenta[operator], x_position, extent_x)
        right_field = lax.dynamic_index_in_dim(fields, displacements[operator], 0, keepdims=False)
        partial_value.append(project(left_field, right_field))
    return jnp.stack(partial_value)

def sandwich_product(sink_elemental, peram_delta, row_start, row_count):
    column_entries = sink_elemental.shape[1]
    real_part = peram_delta[..., :column_entries]
    imag_part = peram_delta[..., column_entries:]
    block_matrix = jnp.concatenate([peram_delta, jnp.concatenate([-imag_part, real_part], axis=-1)], axis=1)
    flat_rows = sink_elemental.reshape(-1, 2 * column_entries)
    mixed_rows = jnp.einsum('mj,ajk->amk', flat_rows.astype(jnp.float32), block_matrix.astype(jnp.float32), precision=lax.Precision.HIGHEST).astype(jnp.bfloat16)
    mixed_rows = mixed_rows.reshape(peram_delta.shape[0], sink_elemental.shape[0], column_entries, 2 * column_entries)
    left_real = lax.dynamic_slice_in_dim(real_part, row_start, row_count, 2)
    left_imag = lax.dynamic_slice_in_dim(imag_part, row_start, row_count, 2)
    mixed_float = mixed_rows.astype(jnp.float32)
    first_factor = jnp.einsum('ail,aoik->olk', left_real.astype(jnp.float32), mixed_float, precision=lax.Precision.HIGHEST)
    second_factor = jnp.einsum('ail,aoik->olk', left_imag.astype(jnp.float32), mixed_float, precision=lax.Precision.HIGHEST)
    sandwich_real = first_factor[..., :column_entries] + second_factor[..., column_entries:]
    sandwich_imaginary = first_factor[..., column_entries:] - second_factor[..., :column_entries]
    return (sandwich_real, sandwich_imaginary)

def contract_meson(incoming_block, sandwich_real, sandwich_imaginary, eigen_total):
    column_entries = sandwich_real.shape[-1]
    incoming_block_float = incoming_block.astype(jnp.float32)
    grand_total = incoming_block_float[..., :column_entries] * sandwich_real + incoming_block_float[..., column_entries:] * sandwich_imaginary
    return lax.optimization_barrier(jnp.sum(grand_total, axis=(1, 2))) / eigen_total

def reference(vectors, gauge_links, perambulators, momenta, displacements):
    norm_factor = 1.0 / math.sqrt(6.0 * SITES)
    x_position = jnp.arange(LX, dtype=jnp.int32).astype(jnp.float32)

    def per_slice(packed):
        vector_slice, link_slice = packed
        fields = smeared_fields(vector_slice, link_slice)
        partial_value = operator_terms(fields, vector_slice, momenta, displacements, x_position, LX)
        return (partial_value * norm_factor).astype(jnp.bfloat16)
    elementals = lax.map(per_slice, (vectors, gauge_links))

    def per_sink(packed):
        slice_index, sink_elemental, perambulator_slice = packed
        earlier = (slice_index - jnp.arange(NDELTA, dtype=jnp.int32)) % NT
        source_times = jnp.take(elementals, earlier.astype(jnp.int32), axis=0)
        correlator_terms = []
        for time_separation in range(NDELTA):
            sandwich_real, sandwich_imaginary = sandwich_product(sink_elemental, perambulator_slice[time_separation], 0, EIGEN_COUNT)
            correlator_terms.append(contract_meson(source_times[time_separation], sandwich_real, sandwich_imaginary, EIGEN_COUNT))
        return jnp.stack(correlator_terms, axis=1)
    correlators = lax.map(per_sink, (jnp.arange(NT, dtype=jnp.int32), elementals, perambulators))
    return (elementals, jnp.transpose(correlators, (1, 0, 2)))
```

```python
import functools
import math

import jax
import jax.numpy as jnp
from jax import lax
from jax.experimental import pallas as pl
from jax.experimental.pallas import tpu as pltpu
from jax.sharding import PartitionSpec as P

F32 = jnp.float32
BF16 = jnp.bfloat16
MESH = pl.DeviceIdType.MESH


def combine(block, n):
    real = block[:n, :n] + block[n:, n:]
    imag = block[:n, n:] - block[n:, :n]
    return real, imag


def field_kernel(disp_ref, v_ref, before_ref, after_ref, links_ref, phase_ref, out_ref, pad, fields, left):
    _, _, nx, ny, nz, n = v_ref.shape
    ops = out_ref.shape[0]
    pad[:, :, 1 : nx + 1] = v_ref[...]
    pad[:, :, 0:1] = before_ref[...]
    pad[:, :, nx + 1 : nx + 2] = after_ref[...]

    def spread(table, column):
        return jnp.broadcast_to(table[:, column : column + 1], (nz, n))

    def load(x, y):
        return [[pad[r, c, x, y].astype(F32) for c in range(3)] for r in range(2)]

    def times(link, field, adjoint):
        real, imag = [], []
        for t in range(3):
            re, im = None, None
            for s in range(3):
                at = s * 3 + t if adjoint else t * 3 + s
                er, ei = link[at], link[9 + at]
                fr, fi = field[0][s], field[1][s]
                if adjoint:
                    a, b = er * fr + ei * fi, er * fi - ei * fr
                else:
                    a, b = er * fr - ei * fi, er * fi + ei * fr
                re = a if re is None else re + a
                im = b if im is None else im + b
            real.append(re)
            imag.append(im)
        return [real, imag]

    def rolled(field, shift):
        return [[pltpu.roll(e, shift, axis=0) for e in part] for part in field]

    def step(i, carry):
        x, y = i // ny, i % ny
        here = load(x + 1, y)
        table = links_ref[x + 1, y]
        back_x = links_ref[x, y]
        y_down = (y + ny - 1) % ny
        back_y = links_ref[x + 1, y_down]
        total = None

        def add(total, field):
            if total is None:
                return field
            return [[a + b for a, b in zip(p, q)] for p, q in zip(total, field)]

        for mu in range(3):
            link = [spread(table, mu * 18 + e) for e in range(18)]
            if mu == 0:
                ahead = load(x + 2, y)
            elif mu == 1:
                ahead = load(x + 1, (y + 1) % ny)
            else:
                ahead = rolled(here, nz - 1)
            forward = times(link, ahead, False)
            total = add(total, forward)
            for r in range(2):
                for c in range(3):
                    fields[mu + 1, c, i, :, r * n : (r + 1) * n] = forward[r][c].astype(BF16)
            if mu == 0:
                behind = [spread(back_x, e) for e in range(18)]
                backward = times(behind, load(x, y), True)
            elif mu == 1:
                behind = [spread(back_y, 18 + e) for e in range(18)]
                backward = times(behind, load(x + 1, y_down), True)
            else:
                backward = rolled(times(link, here, True), 1)
            total = add(total, backward)
        for r in range(2):
            for c in range(3):
                smooth = here[r][c] - total[r][c] / 6.0
                fields[0, c, i, :, r * n : (r + 1) * n] = smooth.astype(BF16)
        angles = phase_ref[x, y]
        for o in range(ops):
            cosine = spread(angles, o)
            sine = spread(angles, ops + o)
            for c in range(3):
                vr, vi = here[0][c], here[1][c]
                left[o, c, i, :, :n] = (vr * cosine - vi * sine).astype(BF16)
                left[o, c, i, :, n:] = (vr * sine + vi * cosine).astype(BF16)
        return carry

    lax.fori_loop(0, nx * ny, step, 0)
    rows = 3 * nx * ny * nz

    def project(o, carry):
        lhs = left[o].reshape(rows, 2 * n)
        rhs = fields[disp_ref[o]].reshape(rows, 2 * n)
        block = lax.dot_general(lhs, rhs, (((0,), (0,)), ((), ())), preferred_element_type=F32)
        real, imag = combine(block, n)
        out_ref[o, :, :n] = real
        out_ref[o, :, n:] = imag
        return carry

    lax.fori_loop(0, ops, project, 0)


def meson_kernel(
    count, norm, part_ref, per_ref, elem_ref, corr_ref,
    got, own, rows_in, ring, mixed, sand, acc, pair_send, pair_recv, send_sem, recv_sem,
):
    seps, spins, n, wide = per_ref.shape
    half = own.shape[0]
    mine_rows = elem_ref.shape[1]
    cfg, t, s = lax.axis_index("cfg"), lax.axis_index("tm"), lax.axis_index("space")
    other = 1 - s
    partner = (cfg, t, other)
    ringed = count == 8 and seps == 8
    if ringed:
        odd = t % 2
        place = (1 - odd) * (t // 2) + odd * ((15 - t) // 2)

        def at_place(p):
            p = (p + 16) % 8
            high = p // 4
            return (1 - high) * (2 * p) + high * (15 - 2 * p)

        targets = [at_place(place + 1), at_place(place - 1)]
        greet = list(targets)
    else:
        targets = [(t + d) % count for d in range(1, seps)]
        greet = targets + [(t + count - d) % count for d in range(1, seps)]

    barrier = pltpu.get_barrier_semaphore()
    pl.semaphore_signal(barrier, inc=1, device_id=partner, device_id_type=MESH)
    for g in greet:
        pl.semaphore_signal(barrier, inc=1, device_id=(cfg, g, s), device_id_type=MESH)
    pl.semaphore_wait(barrier, 1 + len(greet))

    def pair(src, dst, k):
        copy = pltpu.make_async_remote_copy(
            src_ref=src, dst_ref=dst, send_sem=pair_send.at[k], recv_sem=pair_recv.at[k],
            device_id=partner, device_id_type=MESH,
        )
        copy.start()
        return copy

    first = [pair(part_ref.at[other * half + o], got.at[o], o) for o in range(half)]

    if ringed:
        pieces = 2
        size = half // pieces

        def hop(way, k, g):
            span = pl.ds(g * size, size)
            src = own.at[span] if k == 0 else ring.at[way * 4 + k - 1, span]
            return pltpu.make_async_remote_copy(
                src_ref=src, dst_ref=ring.at[way * 4 + k, span],
                send_sem=send_sem.at[way, k, g], recv_sem=recv_sem.at[way, k, g],
                device_id=(cfg, targets[way], s), device_id_type=MESH,
            )

    hops = {}
    for o in range(half):
        first[o].wait_recv()
        own[o] = ((part_ref[s * half + o] + got[o]) * norm).astype(BF16)
        if ringed and (o + 1) % size == 0:
            for way in range(2):
                hops[way, 0, o // size] = hop(way, 0, o // size)
                hops[way, 0, o // size].start()
    if not ringed:
        for k in range(seps - 1):
            hops[k] = pltpu.make_async_remote_copy(
                src_ref=own, dst_ref=ring.at[k], send_sem=send_sem.at[k, 0, 0],
                recv_sem=recv_sem.at[k, 0, 0],
                device_id=(cfg, targets[k], s), device_id_type=MESH,
            )
            hops[k].start()
    rows_copy = pair(own.at[:, pl.ds(other * mine_rows, mine_rows)], rows_in, half)
    elem_ref[pl.ds(s * half, half)] = own[:, pl.ds(s * mine_rows, mine_rows)]

    def sandwich(d):
        flat = own[...].reshape(half * n, wide)
        for a in range(spins):
            spin = per_ref[d, a]
            turned = jnp.concatenate([-spin[:, n:], spin[:, :n]], axis=1)
            block = jnp.concatenate([spin, turned], axis=0)
            prod = jnp.dot(flat, block, preferred_element_type=F32).astype(BF16)
            for o in range(half):
                mixed[a * n : (a + 1) * n, o * wide : (o + 1) * wide] = prod[o * n : (o + 1) * n]
        lhs = per_ref[d].reshape(spins * n, wide).T
        for o in range(half):
            both = jnp.dot(lhs, mixed[:, o * wide : (o + 1) * wide], preferred_element_type=F32)
            real, imag = combine(both, n)
            sand[o, :, :n] = real
            sand[o, :, n:] = imag

    def contract(d, block):
        for o in range(half):
            term = jnp.sum(block[o].astype(F32) * sand[o], axis=0, keepdims=True)
            acc[s, d, pl.ds(o, 1)] = (term[:, :n] + term[:, n:]) * (1.0 / n)

    sandwich(0)
    contract(0, own)
    if ringed:
        for k in range(1, 5):
            for g in range(pieces):
                for way in range(2):
                    if (way, k - 1, g) not in hops or k == 4:
                        continue
                    hops[way, k - 1, g].wait_recv()
                    if k < 3 or g == way:
                        hops[way, k, g] = hop(way, k, g)
                        hops[way, k, g].start()
            if k < 4:
                for way in range(2):
                    source = at_place(place - k if way == 0 else place + k)
                    d = (t - source + 8) % 8
                    sandwich(d)
                    contract(d, ring.at[way * 4 + k - 1])
            else:
                d = (t - at_place(place + 4) + 8) % 8
                sandwich(d)
                hops[0, 3, 0].wait_recv()
                hops[1, 3, 1].wait_recv()
                for o in range(half):
                    way = o // size
                    term = jnp.sum(ring[way * 4 + 3, o].astype(F32) * sand[o], axis=0, keepdims=True)
                    acc[s, d, pl.ds(o, 1)] = (term[:, :n] + term[:, n:]) * (1.0 / n)
    else:
        for k in range(seps - 1):
            sandwich(k + 1)
            hops[k].wait_recv()
            contract(k + 1, ring.at[k])
    last = pair(acc.at[s], acc.at[s], half + 1)
    rows_copy.wait_recv()
    elem_ref[pl.ds(other * half, half)] = rows_in[...]
    for copy in hops.values():
        copy.wait_send()
    for copy in first:
        copy.wait_send()
    rows_copy.wait_send()
    last.wait()
    corr_ref[...] = acc[...]


def body(vectors, gauge_links, perambulators, momenta, displacements):
    space_index = lax.axis_index("space")
    space_count = lax.axis_size("space")
    count = lax.axis_size("tm")
    field = vectors[0]
    _, _, nx, ny, nz, n = field.shape
    ops = momenta.shape[0]
    up = [(i, (i + 1) % space_count) for i in range(space_count)]
    down = [(j, i) for i, j in up]
    before = lax.ppermute(field[:, :, nx - 1 :], "space", up)
    after = lax.ppermute(field[:, :, :1], "space", down)
    links = gauge_links[0]
    lower = lax.ppermute(links[0, :, :, :, nx - 1 :], "space", up)
    lower = jnp.concatenate([lower[None], jnp.zeros((2,) + lower.shape, F32)])
    links = jnp.concatenate([lower, links], axis=4)
    links = jnp.transpose(links.reshape(54, nx + 1, ny, nz), (1, 2, 3, 0))

    extent_x = nx * space_count
    xs = (space_index * nx + jnp.arange(nx, dtype=jnp.int32)).astype(F32)
    ys = jnp.arange(ny, dtype=jnp.int32).astype(F32)
    zs = jnp.arange(nz, dtype=jnp.int32).astype(F32)
    mom = momenta.astype(F32)
    angle = (mom[:, 0] * xs[:, None] / extent_x)[:, None, None, :]
    angle = angle + (mom[:, 1] * ys[:, None] / ny)[None, :, None, :]
    angle = angle + (mom[:, 2] * zs[:, None] / nz)[None, None, :, :]
    angle = 2.0 * math.pi * angle
    phases = jnp.concatenate([jnp.cos(angle), jnp.sin(angle)], axis=-1)

    vmem = pl.BlockSpec(memory_space=pltpu.VMEM)
    partial_value = pl.pallas_call(
        field_kernel,
        out_shape=jax.ShapeDtypeStruct((ops, n, 2 * n), F32),
        in_specs=[pl.BlockSpec(memory_space=pltpu.SMEM)] + [vmem] * 5,
        out_specs=vmem,
        scratch_shapes=[
            pltpu.VMEM((2, 3, nx + 2, ny, nz, n), BF16),
            pltpu.VMEM((4, 3, nx * ny, nz, 2 * n), BF16),
            pltpu.VMEM((ops, 3, nx * ny, nz, 2 * n), BF16),
        ],
        compiler_params=pltpu.CompilerParams(vmem_limit_bytes=40 * 2**20),
        name="fields",
    )(displacements, field, before, after, links, phases)

    perams = perambulators[0]
    seps, spins = perams.shape[:2]
    half = ops // 2
    norm = 1.0 / math.sqrt(6.0 * extent_x * ny * nz)
    elementals, corr = pl.pallas_call(
        functools.partial(meson_kernel, count, norm),
        out_shape=(
            jax.ShapeDtypeStruct((ops, n // 2, 2 * n), BF16),
            jax.ShapeDtypeStruct((2, seps, half, n), F32),
        ),
        in_specs=[vmem] * 2,
        out_specs=(vmem, vmem),
        scratch_shapes=[
            pltpu.VMEM((half, n, 2 * n), F32),
            pltpu.VMEM((half, n, 2 * n), BF16),
            pltpu.VMEM((half, n // 2, 2 * n), BF16),
            pltpu.VMEM((8, half, n, 2 * n), BF16),
            pltpu.VMEM((spins * n, half * 2 * n), BF16),
            pltpu.VMEM((half, n, 2 * n), F32),
            pltpu.VMEM((2, seps, half, n), F32),
            pltpu.SemaphoreType.DMA((half + 2,)),
            pltpu.SemaphoreType.DMA((half + 2,)),
            pltpu.SemaphoreType.DMA((8, 4, 2)),
            pltpu.SemaphoreType.DMA((8, 4, 2)),
        ],
        compiler_params=pltpu.CompilerParams(
            collective_id=0, has_side_effects=True, vmem_limit_bytes=40 * 2**20
        ),
        name="mesons",
    )(partial_value, perams)
    corr = jnp.sum(corr, axis=-1)
    corr = jnp.transpose(corr, (0, 2, 1)).reshape(ops, 1, seps)
    return (elementals[None], corr)


def solution(mesh):
    return jax.shard_map(
        body,
        mesh=mesh,
        in_specs=(
            P(("cfg", "tm"), None, None, "space", None, None, None),
            P(("cfg", "tm"), None, None, None, None, "space", None, None),
            P(("cfg", "tm"), None, None, None, None),
            P(),
            P(),
        ),
        out_specs=(P(("cfg", "tm"), None, "space", None), P(None, ("cfg", "tm"), None)),
        check_vma=False,
    )
```

```python
import functools
import math

import jax
import jax.numpy as jnp
from jax import lax
from jax.experimental import pallas as pl
from jax.experimental.pallas import tpu as pltpu
from jax.sharding import PartitionSpec as P

F32 = jnp.float32
BF16 = jnp.bfloat16
MESH = pl.DeviceIdType.MESH


def combine(block, n):
    real = block[:n, :n] + block[n:, n:]
    imag = block[:n, n:] - block[n:, :n]
    return real, imag


def make_fields(ready, v_ref, phase_ref, links_ref, pad, fields, left):
    _, _, nx, ny, nz, n = v_ref.shape
    ops = left.shape[0]

    def spread(table, column):
        return jnp.broadcast_to(table[:, column : column + 1], (nz, n))

    def load(x, y):
        return [[pad[r, c, x, y].astype(F32) for c in range(3)] for r in range(2)]

    def times(link, field, adjoint):
        real, imag = [], []
        for t in range(3):
            re, im = None, None
            for s in range(3):
                at = s * 3 + t if adjoint else t * 3 + s
                er, ei = link[at], link[9 + at]
                fr, fi = field[0][s], field[1][s]
                if adjoint:
                    a, b = er * fr + ei * fi, er * fi - ei * fr
                else:
                    a, b = er * fr - ei * fi, er * fi + ei * fr
                re = a if re is None else re + a
                im = b if im is None else im + b
            real.append(re)
            imag.append(im)
        return [real, imag]

    def rolled(field, shift):
        return [[pltpu.roll(e, shift, axis=0) for e in part] for part in field]

    def step(i, carry):
        x, y = i // ny, i % ny
        here = load(x + 1, y)
        table = links_ref[x + 1, y]
        back_x = links_ref[x, y]
        y_down = (y + ny - 1) % ny
        back_y = links_ref[x + 1, y_down]
        total = None

        def add(total, field):
            if total is None:
                return field
            return [[a + b for a, b in zip(p, q)] for p, q in zip(total, field)]

        for mu in range(3):
            link = [spread(table, mu * 18 + e) for e in range(18)]
            if mu == 0:
                ahead = load(x + 2, y)
            elif mu == 1:
                ahead = load(x + 1, (y + 1) % ny)
            else:
                ahead = rolled(here, nz - 1)
            forward = times(link, ahead, False)
            total = add(total, forward)
            for r in range(2):
                for c in range(3):
                    fields[mu + 1, c, i, :, r * n : (r + 1) * n] = forward[r][c].astype(BF16)
            if mu == 0:
                behind = [spread(back_x, e) for e in range(18)]
                backward = times(behind, load(x, y), True)
            elif mu == 1:
                behind = [spread(back_y, 18 + e) for e in range(18)]
                backward = times(behind, load(x + 1, y_down), True)
            else:
                backward = rolled(times(link, here, True), 1)
            total = add(total, backward)
        for r in range(2):
            for c in range(3):
                smooth = here[r][c] - total[r][c] / 6.0
                fields[0, c, i, :, r * n : (r + 1) * n] = smooth.astype(BF16)
        return carry

    def rotate(i, carry):
        x, y = i // ny, i % ny
        angles = phase_ref[x, y]
        for o in range(ops):
            cosine = spread(angles, o)
            sine = spread(angles, ops + o)
            for c in range(3):
                vr, vi = v_ref[0, c, x, y].astype(F32), v_ref[1, c, x, y].astype(F32)
                left[o, c, i, :, :n] = (vr * cosine - vi * sine).astype(BF16)
                left[o, c, i, :, n:] = (vr * sine + vi * cosine).astype(BF16)
        return carry

    lax.fori_loop(0, nx * ny, rotate, 0)
    ready()
    lax.fori_loop(0, nx * ny, step, 0)


def meson_kernel(
    count, norm, disp_ref, v_ref, link_ref, phase_ref, per_ref, elem_ref, corr_ref,
    pad, links, fields, left, part, got, own, rows_in, ring, mixed, sand, acc, pair_send, pair_recv, send_sem, recv_sem,
):
    seps, spins, n, wide = per_ref.shape
    half = own.shape[0]
    mine_rows = elem_ref.shape[1]
    cfg, t, s = lax.axis_index("cfg"), lax.axis_index("tm"), lax.axis_index("space")
    other = 1 - s
    partner = (cfg, t, other)
    ringed = count == 8 and seps == 8
    if ringed:
        odd = t % 2
        place = (1 - odd) * (t // 2) + odd * ((15 - t) // 2)

        def at_place(p):
            p = (p + 16) % 8
            high = p // 4
            return (1 - high) * (2 * p) + high * (15 - 2 * p)

        targets = [at_place(place + 1), at_place(place - 1)]
        greet = list(targets)
    else:
        targets = [(t + d) % count for d in range(1, seps)]
        greet = targets + [(t + count - d) % count for d in range(1, seps)]

    barrier = pltpu.get_barrier_semaphore()
    pl.semaphore_signal(barrier, inc=1, device_id=partner, device_id_type=MESH)
    for g in greet:
        pl.semaphore_signal(barrier, inc=1, device_id=(cfg, g, s), device_id_type=MESH)
    pl.semaphore_wait(barrier, 1 + len(greet))

    def pair(src, dst, k):
        copy = pltpu.make_async_remote_copy(
            src_ref=src, dst_ref=dst, send_sem=pair_send.at[k], recv_sem=pair_recv.at[k],
            device_id=partner, device_id_type=MESH,
        )
        copy.start()
        return copy

    nx = v_ref.shape[2]
    rows = fields.shape[1] * fields.shape[2] * fields.shape[3]
    halo = [
        pair(v_ref.at[:, :, nx - 1], pad.at[:, :, 0], half + 2),
        pair(v_ref.at[:, :, 0], pad.at[:, :, nx + 1], half + 3),
        pair(link_ref.at[nx - 1], links.at[0], half + 4),
    ]
    pad[:, :, 1 : nx + 1] = v_ref[...]
    links[1:] = link_ref[...]

    def ready():
        for copy in halo:
            copy.wait_recv()

    make_fields(ready, v_ref, phase_ref, links, pad, fields, left)

    def project(o):
        lhs = left[o].reshape(rows, wide)
        rhs = fields[disp_ref[o]].reshape(rows, wide)
        block = lax.dot_general(lhs, rhs, (((0,), (0,)), ((), ())), preferred_element_type=F32)
        return combine(block, n)

    first = []
    for o in range(half):
        part[o, :, :n], part[o, :, n:] = project(other * half + o)
        first.append(pair(part.at[o], got.at[o], o))

    if ringed:
        pieces = 2
        size = half // pieces

        def hop(way, k, g):
            span = pl.ds(g * size, size)
            src = own.at[span] if k == 0 else ring.at[way * 4 + k - 1, span]
            return pltpu.make_async_remote_copy(
                src_ref=src, dst_ref=ring.at[way * 4 + k, span],
                send_sem=send_sem.at[way, k, g], recv_sem=recv_sem.at[way, k, g],
                device_id=(cfg, targets[way], s), device_id_type=MESH,
            )

    hops = {}
    for o in range(half):
        real, imag = project(s * half + o)
        first[o].wait_recv()
        own[o, :, :n] = ((real + got[o, :, :n]) * norm).astype(BF16)
        own[o, :, n:] = ((imag + got[o, :, n:]) * norm).astype(BF16)
        if ringed and (o + 1) % size == 0:
            for way in range(2):
                hops[way, 0, o // size] = hop(way, 0, o // size)
                hops[way, 0, o // size].start()
    if not ringed:
        for k in range(seps - 1):
            hops[k] = pltpu.make_async_remote_copy(
                src_ref=own, dst_ref=ring.at[k], send_sem=send_sem.at[k, 0, 0],
                recv_sem=recv_sem.at[k, 0, 0],
                device_id=(cfg, targets[k], s), device_id_type=MESH,
            )
            hops[k].start()
    rows_copy = pair(own.at[:, pl.ds(other * mine_rows, mine_rows)], rows_in, half)
    elem_ref[pl.ds(s * half, half)] = own[:, pl.ds(s * mine_rows, mine_rows)]

    def sandwich(d):
        flat = own[...].reshape(half * n, wide)
        for a in range(spins):
            spin = per_ref[d, a]
            turned = jnp.concatenate([-spin[:, n:], spin[:, :n]], axis=1)
            block = jnp.concatenate([spin, turned], axis=0)
            prod = jnp.dot(flat, block, preferred_element_type=F32).astype(BF16)
            for o in range(half):
                mixed[a * n : (a + 1) * n, o * wide : (o + 1) * wide] = prod[o * n : (o + 1) * n]
        lhs = per_ref[d].reshape(spins * n, wide).T
        for o in range(half):
            both = jnp.dot(lhs, mixed[:, o * wide : (o + 1) * wide], preferred_element_type=F32)
            real, imag = combine(both, n)
            sand[o, :, :n] = real
            sand[o, :, n:] = imag

    def contract(d, block):
        for o in range(half):
            term = jnp.sum(block[o].astype(F32) * sand[o], axis=0, keepdims=True)
            acc[s, d, pl.ds(o, 1)] = (term[:, :n] + term[:, n:]) * (1.0 / n)

    sandwich(0)
    contract(0, own)
    if ringed:
        for k in range(1, 5):
            for g in range(pieces):
                for way in range(2):
                    if (way, k - 1, g) not in hops or k == 4:
                        continue
                    hops[way, k - 1, g].wait_recv()
                    if k < 3 or g == way:
                        hops[way, k, g] = hop(way, k, g)
                        hops[way, k, g].start()
            if k < 4:
                for way in range(2):
                    source = at_place(place - k if way == 0 else place + k)
                    d = (t - source + 8) % 8
                    sandwich(d)
                    contract(d, ring.at[way * 4 + k - 1])
            else:
                d = (t - at_place(place + 4) + 8) % 8
                sandwich(d)
                hops[0, 3, 0].wait_recv()
                hops[1, 3, 1].wait_recv()
                for o in range(half):
                    way = o // size
                    term = jnp.sum(ring[way * 4 + 3, o].astype(F32) * sand[o], axis=0, keepdims=True)
                    acc[s, d, pl.ds(o, 1)] = (term[:, :n] + term[:, n:]) * (1.0 / n)
    else:
        for k in range(seps - 1):
            sandwich(k + 1)
            hops[k].wait_recv()
            contract(k + 1, ring.at[k])
    last = pair(acc.at[s], acc.at[s], half + 1)
    rows_copy.wait_recv()
    elem_ref[pl.ds(other * half, half)] = rows_in[...]
    for copy in hops.values():
        copy.wait_send()
    for copy in halo + first:
        copy.wait_send()
    rows_copy.wait_send()
    last.wait()
    corr_ref[...] = acc[...]


def body(vectors, gauge_links, perambulators, momenta, displacements):
    space_index = lax.axis_index("space")
    space_count = lax.axis_size("space")
    count = lax.axis_size("tm")
    field = vectors[0]
    _, _, nx, ny, nz, n = field.shape
    ops = momenta.shape[0]
    links = gauge_links[0]
    links = jnp.transpose(links.reshape(54, nx, ny, nz), (1, 2, 3, 0))

    extent_x = nx * space_count
    xs = (space_index * nx + jnp.arange(nx, dtype=jnp.int32)).astype(F32)
    ys = jnp.arange(ny, dtype=jnp.int32).astype(F32)
    zs = jnp.arange(nz, dtype=jnp.int32).astype(F32)
    mom = momenta.astype(F32)
    angle = (mom[:, 0] * xs[:, None] / extent_x)[:, None, None, :]
    angle = angle + (mom[:, 1] * ys[:, None] / ny)[None, :, None, :]
    angle = angle + (mom[:, 2] * zs[:, None] / nz)[None, None, :, :]
    angle = 2.0 * math.pi * angle
    phases = jnp.concatenate([jnp.cos(angle), jnp.sin(angle)], axis=-1)

    vmem = pl.BlockSpec(memory_space=pltpu.VMEM)
    perams = perambulators[0]
    seps, spins = perams.shape[:2]
    half = ops // 2
    norm = 1.0 / math.sqrt(6.0 * extent_x * ny * nz)
    elementals, corr = pl.pallas_call(
        functools.partial(meson_kernel, count, norm),
        out_shape=(
            jax.ShapeDtypeStruct((ops, n // 2, 2 * n), BF16),
            jax.ShapeDtypeStruct((2, seps, half, n), F32),
        ),
        in_specs=[pl.BlockSpec(memory_space=pltpu.SMEM)] + [vmem] * 4,
        out_specs=(vmem, vmem),
        scratch_shapes=[
            pltpu.VMEM((2, 3, nx + 2, ny, nz, n), BF16),
            pltpu.VMEM((nx + 1, ny, nz, 54), F32),
            pltpu.VMEM((4, 3, nx * ny, nz, 2 * n), BF16),
            pltpu.VMEM((ops, 3, nx * ny, nz, 2 * n), BF16),
            pltpu.VMEM((half, n, 2 * n), F32),
            pltpu.VMEM((half, n, 2 * n), F32),
            pltpu.VMEM((half, n, 2 * n), BF16),
            pltpu.VMEM((half, n // 2, 2 * n), BF16),
            pltpu.VMEM((8, half, n, 2 * n), BF16),
            pltpu.VMEM((spins * n, half * 2 * n), BF16),
            pltpu.VMEM((half, n, 2 * n), F32),
            pltpu.VMEM((2, seps, half, n), F32),
            pltpu.SemaphoreType.DMA((half + 5,)),
            pltpu.SemaphoreType.DMA((half + 5,)),
            pltpu.SemaphoreType.DMA((8, 4, 2)),
            pltpu.SemaphoreType.DMA((8, 4, 2)),
        ],
        compiler_params=pltpu.CompilerParams(
            collective_id=0, has_side_effects=True, vmem_limit_bytes=40 * 2**20
        ),
        name="mesons",
    )(displacements, field, links, phases, perams)
    corr = jnp.sum(corr, axis=-1)
    corr = jnp.transpose(corr, (0, 2, 1)).reshape(ops, 1, seps)
    return (elementals[None], corr)


def solution(mesh):
    return jax.shard_map(
        body,
        mesh=mesh,
        in_specs=(
            P(("cfg", "tm"), None, None, "space", None, None, None),
            P(("cfg", "tm"), None, None, None, None, "space", None, None),
            P(("cfg", "tm"), None, None, None, None),
            P(),
            P(),
        ),
        out_specs=(P(("cfg", "tm"), None, "space", None), P(None, ("cfg", "tm"), None)),
        check_vma=False,
    )
```

```python
import functools
import math

import jax
import jax.numpy as jnp
from jax import lax
from jax.experimental import pallas as pl
from jax.experimental.pallas import tpu as pltpu
from jax.sharding import PartitionSpec as P

F32 = jnp.float32
BF16 = jnp.bfloat16
MESH = pl.DeviceIdType.MESH


def combine(block, n):
    real = block[:n, :n] + block[n:, n:]
    imag = block[:n, n:] - block[n:, :n]
    return real, imag


def make_fields(ready, v_ref, phase_ref, links_ref, pad, fields, left):
    _, _, nx, ny, nz, n = v_ref.shape
    ops = left.shape[0]

    def spread(table, column):
        return jnp.broadcast_to(table[:, column : column + 1], (nz, n))

    def load(x, y):
        return [[pad[r, c, x, y].astype(F32) for c in range(3)] for r in range(2)]

    def times(link, field, adjoint):
        real, imag = [], []
        for t in range(3):
            re, im = None, None
            for s in range(3):
                at = s * 3 + t if adjoint else t * 3 + s
                er, ei = link[at], link[9 + at]
                fr, fi = field[0][s], field[1][s]
                if adjoint:
                    a, b = er * fr + ei * fi, er * fi - ei * fr
                else:
                    a, b = er * fr - ei * fi, er * fi + ei * fr
                re = a if re is None else re + a
                im = b if im is None else im + b
            real.append(re)
            imag.append(im)
        return [real, imag]

    def rolled(field, shift):
        return [[pltpu.roll(e, shift, axis=0) for e in part] for part in field]

    def step(i, carry):
        x, y = i // ny, i % ny
        here = load(x + 1, y)
        table = links_ref[x + 1, y]
        back_x = links_ref[x, y]
        y_down = (y + ny - 1) % ny
        back_y = links_ref[x + 1, y_down]
        total = None

        def add(total, field):
            if total is None:
                return field
            return [[a + b for a, b in zip(p, q)] for p, q in zip(total, field)]

        for mu in range(3):
            link = [spread(table, mu * 18 + e) for e in range(18)]
            if mu == 0:
                ahead = load(x + 2, y)
            elif mu == 1:
                ahead = load(x + 1, (y + 1) % ny)
            else:
                ahead = rolled(here, nz - 1)
            forward = times(link, ahead, False)
            total = add(total, forward)
            for r in range(2):
                for c in range(3):
                    fields[mu + 1, c, i, :, r * n : (r + 1) * n] = forward[r][c].astype(BF16)
            if mu == 0:
                behind = [spread(back_x, e) for e in range(18)]
                backward = times(behind, load(x, y), True)
            elif mu == 1:
                behind = [spread(back_y, 18 + e) for e in range(18)]
                backward = times(behind, load(x + 1, y_down), True)
            else:
                backward = rolled(times(link, here, True), 1)
            total = add(total, backward)
        for r in range(2):
            for c in range(3):
                smooth = here[r][c] - total[r][c] / 6.0
                fields[0, c, i, :, r * n : (r + 1) * n] = smooth.astype(BF16)
        return carry

    def rotate(i, carry):
        x, y = i // ny, i % ny
        angles = phase_ref[x, y]
        for o in range(ops):
            cosine = spread(angles, o)
            sine = spread(angles, ops + o)
            for c in range(3):
                vr, vi = v_ref[0, c, x, y].astype(F32), v_ref[1, c, x, y].astype(F32)
                left[o, c, i, :, :n] = (vr * cosine - vi * sine).astype(BF16)
                left[o, c, i, :, n:] = (vr * sine + vi * cosine).astype(BF16)
        return carry

    lax.fori_loop(0, nx * ny, rotate, 0)
    ready()
    lax.fori_loop(0, nx * ny, step, 0)


def meson_kernel(
    count, norm, disp_ref, v_ref, link_ref, phase_ref, per_hbm, elem_ref, corr_ref,
    pad, links, fields, left, part, got, own, rows_in, ring, mixed, sand, acc, per_ref, per_sem, pair_send, pair_recv, send_sem, recv_sem,
):
    seps, spins, n, wide = per_ref.shape
    fetch = pltpu.make_async_copy(per_hbm, per_ref, per_sem)
    fetch.start()
    half = own.shape[0]
    mine_rows = elem_ref.shape[1]
    cfg, t, s = lax.axis_index("cfg"), lax.axis_index("tm"), lax.axis_index("space")
    other = 1 - s
    partner = (cfg, t, other)
    ringed = count == 8 and seps == 8
    if ringed:
        odd = t % 2
        place = (1 - odd) * (t // 2) + odd * ((15 - t) // 2)

        def at_place(p):
            p = (p + 16) % 8
            high = p // 4
            return (1 - high) * (2 * p) + high * (15 - 2 * p)

        targets = [at_place(place + 1), at_place(place - 1)]
        greet = list(targets)
    else:
        targets = [(t + d) % count for d in range(1, seps)]
        greet = targets + [(t + count - d) % count for d in range(1, seps)]

    barrier = pltpu.get_barrier_semaphore()
    pl.semaphore_signal(barrier, inc=1, device_id=partner, device_id_type=MESH)
    for g in greet:
        pl.semaphore_signal(barrier, inc=1, device_id=(cfg, g, s), device_id_type=MESH)
    pl.semaphore_wait(barrier, 1 + len(greet))

    def pair(src, dst, k):
        copy = pltpu.make_async_remote_copy(
            src_ref=src, dst_ref=dst, send_sem=pair_send.at[k], recv_sem=pair_recv.at[k],
            device_id=partner, device_id_type=MESH,
        )
        copy.start()
        return copy

    nx = v_ref.shape[2]
    rows = fields.shape[1] * fields.shape[2] * fields.shape[3]
    halo = [
        pair(v_ref.at[:, :, nx - 1], pad.at[:, :, 0], half + 2),
        pair(v_ref.at[:, :, 0], pad.at[:, :, nx + 1], half + 3),
        pair(link_ref.at[nx - 1], links.at[0], half + 4),
    ]
    pad[:, :, 1 : nx + 1] = v_ref[...]
    links[1:] = link_ref[...]

    def ready():
        for copy in halo:
            copy.wait_recv()

    make_fields(ready, v_ref, phase_ref, links, pad, fields, left)

    def project(o):
        lhs = left[o].reshape(rows, wide)
        rhs = fields[disp_ref[o]].reshape(rows, wide)
        block = lax.dot_general(lhs, rhs, (((0,), (0,)), ((), ())), preferred_element_type=F32)
        return combine(block, n)

    first = []

    def project_other(o):
        part[o, :, :n], part[o, :, n:] = project(other * half + o)
        first.append(pair(part.at[o], got.at[o], o))

    project_other(0)

    if ringed:
        pieces = half
        size = half // pieces

        def hop(way, k, g):
            span = pl.ds(g * size, size)
            src = own.at[span] if k == 0 else ring.at[way * 4 + k - 1, span]
            return pltpu.make_async_remote_copy(
                src_ref=src, dst_ref=ring.at[way * 4 + k, span],
                send_sem=send_sem.at[way, k, g], recv_sem=recv_sem.at[way, k, g],
                device_id=(cfg, targets[way], s), device_id_type=MESH,
            )

    hops = {}
    for o in range(half):
        if o + 1 < half:
            project_other(o + 1)
        real, imag = project(s * half + o)
        first[o].wait_recv()
        own[o, :, :n] = ((real + got[o, :, :n]) * norm).astype(BF16)
        own[o, :, n:] = ((imag + got[o, :, n:]) * norm).astype(BF16)
        if ringed and (o + 1) % size == 0:
            for way in range(2):
                hops[way, 0, o // size] = hop(way, 0, o // size)
                hops[way, 0, o // size].start()
    if not ringed:
        for k in range(seps - 1):
            hops[k] = pltpu.make_async_remote_copy(
                src_ref=own, dst_ref=ring.at[k], send_sem=send_sem.at[k, 0, 0],
                recv_sem=recv_sem.at[k, 0, 0],
                device_id=(cfg, targets[k], s), device_id_type=MESH,
            )
            hops[k].start()
    rows_copy = pair(own.at[:, pl.ds(other * mine_rows, mine_rows)], rows_in, half)
    elem_ref[pl.ds(s * half, half)] = own[:, pl.ds(s * mine_rows, mine_rows)]

    def sandwich(d):
        flat = own[...].reshape(half * n, wide)
        for a in range(spins):
            spin = per_ref[d, a]
            turned = jnp.concatenate([-spin[:, n:], spin[:, :n]], axis=1)
            block = jnp.concatenate([spin, turned], axis=0)
            prod = jnp.dot(flat, block, preferred_element_type=F32).astype(BF16)
            for o in range(half):
                mixed[a * n : (a + 1) * n, o * wide : (o + 1) * wide] = prod[o * n : (o + 1) * n]
        lhs = per_ref[d].reshape(spins * n, wide).T
        for o in range(half):
            both = jnp.dot(lhs, mixed[:, o * wide : (o + 1) * wide], preferred_element_type=F32)
            real, imag = combine(both, n)
            sand[o, :, :n] = real
            sand[o, :, n:] = imag

    def contract(d, block):
        for o in range(half):
            term = jnp.sum(block[o].astype(F32) * sand[o], axis=0, keepdims=True)
            acc[s, d, pl.ds(o, 1)] = (term[:, :n] + term[:, n:]) * (1.0 / n)

    fetch.wait()
    sandwich(0)
    contract(0, own)
    if ringed:
        for k in range(1, 5):
            for g in range(pieces):
                for way in range(2):
                    if (way, k - 1, g) not in hops or k == 4:
                        continue
                    hops[way, k - 1, g].wait_recv()
                    if k < 3 or g // 2 == way:
                        hops[way, k, g] = hop(way, k, g)
                        hops[way, k, g].start()
            if k < 4:
                for way in range(2):
                    source = at_place(place - k if way == 0 else place + k)
                    d = (t - source + 8) % 8
                    sandwich(d)
                    contract(d, ring.at[way * 4 + k - 1])
            else:
                d = (t - at_place(place + 4) + 8) % 8
                sandwich(d)
                for o in range(half):
                    way = o // 2
                    hops[way, 3, o].wait_recv()
                    term = jnp.sum(ring[way * 4 + 3, o].astype(F32) * sand[o], axis=0, keepdims=True)
                    acc[s, d, pl.ds(o, 1)] = (term[:, :n] + term[:, n:]) * (1.0 / n)
    else:
        for k in range(seps - 1):
            sandwich(k + 1)
            hops[k].wait_recv()
            contract(k + 1, ring.at[k])
    last = pair(acc.at[s], acc.at[s], half + 1)
    rows_copy.wait_recv()
    elem_ref[pl.ds(other * half, half)] = rows_in[...]
    for copy in hops.values():
        copy.wait_send()
    for copy in halo + first:
        copy.wait_send()
    rows_copy.wait_send()
    last.wait()
    corr_ref[...] = acc[...]


def body(vectors, gauge_links, perambulators, momenta, displacements):
    space_index = lax.axis_index("space")
    space_count = lax.axis_size("space")
    count = lax.axis_size("tm")
    field = vectors[0]
    _, _, nx, ny, nz, n = field.shape
    ops = momenta.shape[0]
    links = gauge_links[0]
    links = jnp.transpose(links.reshape(54, nx, ny, nz), (1, 2, 3, 0))

    extent_x = nx * space_count
    xs = (space_index * nx + jnp.arange(nx, dtype=jnp.int32)).astype(F32)
    ys = jnp.arange(ny, dtype=jnp.int32).astype(F32)
    zs = jnp.arange(nz, dtype=jnp.int32).astype(F32)
    mom = momenta.astype(F32)
    angle = (mom[:, 0] * xs[:, None] / extent_x)[:, None, None, :]
    angle = angle + (mom[:, 1] * ys[:, None] / ny)[None, :, None, :]
    angle = angle + (mom[:, 2] * zs[:, None] / nz)[None, None, :, :]
    angle = 2.0 * math.pi * angle
    phases = jnp.concatenate([jnp.cos(angle), jnp.sin(angle)], axis=-1)

    vmem = pl.BlockSpec(memory_space=pltpu.VMEM)
    perams = perambulators[0]
    seps, spins = perams.shape[:2]
    half = ops // 2
    norm = 1.0 / math.sqrt(6.0 * extent_x * ny * nz)
    elementals, corr = pl.pallas_call(
        functools.partial(meson_kernel, count, norm),
        out_shape=(
            jax.ShapeDtypeStruct((ops, n // 2, 2 * n), BF16),
            jax.ShapeDtypeStruct((2, seps, half, n), F32),
        ),
        in_specs=[pl.BlockSpec(memory_space=pltpu.SMEM)] + [vmem] * 3 + [pl.BlockSpec(memory_space=pl.ANY)],
        out_specs=(vmem, vmem),
        scratch_shapes=[
            pltpu.VMEM((2, 3, nx + 2, ny, nz, n), BF16),
            pltpu.VMEM((nx + 1, ny, nz, 54), F32),
            pltpu.VMEM((4, 3, nx * ny, nz, 2 * n), BF16),
            pltpu.VMEM((ops, 3, nx * ny, nz, 2 * n), BF16),
            pltpu.VMEM((half, n, 2 * n), F32),
            pltpu.VMEM((half, n, 2 * n), F32),
            pltpu.VMEM((half, n, 2 * n), BF16),
            pltpu.VMEM((half, n // 2, 2 * n), BF16),
            pltpu.VMEM((8, half, n, 2 * n), BF16),
            pltpu.VMEM((spins * n, half * 2 * n), BF16),
            pltpu.VMEM((half, n, 2 * n), F32),
            pltpu.VMEM((2, seps, half, n), F32),
            pltpu.VMEM(perams.shape, BF16),
            pltpu.SemaphoreType.DMA,
            pltpu.SemaphoreType.DMA((half + 5,)),
            pltpu.SemaphoreType.DMA((half + 5,)),
            pltpu.SemaphoreType.DMA((8, 4, half)),
            pltpu.SemaphoreType.DMA((8, 4, half)),
        ],
        compiler_params=pltpu.CompilerParams(
            collective_id=0, has_side_effects=True, vmem_limit_bytes=48 * 2**20
        ),
        name="mesons",
    )(displacements, field, links, phases, perams)
    corr = jnp.sum(corr, axis=-1)
    corr = jnp.transpose(corr, (0, 2, 1)).reshape(ops, 1, seps)
    return (elementals[None], corr)


def solution(mesh):
    return jax.shard_map(
        body,
        mesh=mesh,
        in_specs=(
            P(("cfg", "tm"), None, None, "space", None, None, None),
            P(("cfg", "tm"), None, None, None, None, "space", None, None),
            P(("cfg", "tm"), None, None, None, None),
            P(),
            P(),
        ),
        out_specs=(P(("cfg", "tm"), None, "space", None), P(None, ("cfg", "tm"), None)),
        check_vma=False,
    )
```

```python
import functools
import math

import jax
import jax.numpy as jnp
from jax import lax
from jax.experimental import pallas as pl
from jax.experimental.pallas import tpu as pltpu
from jax.sharding import PartitionSpec as P

F32 = jnp.float32
BF16 = jnp.bfloat16
MESH = pl.DeviceIdType.MESH


def combine(block, n):
    real = block[:n, :n] + block[n:, n:]
    imag = block[:n, n:] - block[n:, :n]
    return real, imag


def make_fields(ready, v_ref, phase_ref, links_ref, pad, fields, left):
    _, _, nx, ny, nz, n = v_ref.shape
    ops = left.shape[0]

    def spread(table, column):
        return jnp.broadcast_to(table[:, column : column + 1], (nz, n))

    def load(x, y):
        return [[pad[r, c, x, y].astype(F32) for c in range(3)] for r in range(2)]

    def times(link, field, adjoint):
        real, imag = [], []
        for t in range(3):
            re, im = None, None
            for s in range(3):
                at = s * 3 + t if adjoint else t * 3 + s
                er, ei = link[at], link[9 + at]
                fr, fi = field[0][s], field[1][s]
                if adjoint:
                    a, b = er * fr + ei * fi, er * fi - ei * fr
                else:
                    a, b = er * fr - ei * fi, er * fi + ei * fr
                re = a if re is None else re + a
                im = b if im is None else im + b
            real.append(re)
            imag.append(im)
        return [real, imag]

    def rolled(field, shift):
        return [[pltpu.roll(e, shift, axis=0) for e in part] for part in field]

    def step(i, carry):
        x, y = i // ny, i % ny
        here = load(x + 1, y)
        table = links_ref[x + 1, y]
        back_x = links_ref[x, y]
        y_down = (y + ny - 1) % ny
        back_y = links_ref[x + 1, y_down]
        total = None

        def add(total, field):
            if total is None:
                return field
            return [[a + b for a, b in zip(p, q)] for p, q in zip(total, field)]

        for mu in range(3):
            link = [spread(table, mu * 18 + e) for e in range(18)]
            if mu == 0:
                ahead = load(x + 2, y)
            elif mu == 1:
                ahead = load(x + 1, (y + 1) % ny)
            else:
                ahead = rolled(here, nz - 1)
            forward = times(link, ahead, False)
            total = add(total, forward)
            for r in range(2):
                for c in range(3):
                    fields[mu + 1, c, i, :, r * n : (r + 1) * n] = forward[r][c].astype(BF16)
            if mu == 0:
                behind = [spread(back_x, e) for e in range(18)]
                backward = times(behind, load(x, y), True)
            elif mu == 1:
                behind = [spread(back_y, 18 + e) for e in range(18)]
                backward = times(behind, load(x + 1, y_down), True)
            else:
                backward = rolled(times(link, here, True), 1)
            total = add(total, backward)
        for r in range(2):
            for c in range(3):
                smooth = here[r][c] - total[r][c] / 6.0
                fields[0, c, i, :, r * n : (r + 1) * n] = smooth.astype(BF16)
        return carry

    def rotate(i, carry):
        x, y = i // ny, i % ny
        angles = phase_ref[x, y]
        for o in range(ops):
            cosine = spread(angles, o)
            sine = spread(angles, ops + o)
            for c in range(3):
                vr, vi = pad[0, c, x + 1, y].astype(F32), pad[1, c, x + 1, y].astype(F32)
                left[o, c, i, :, :n] = (vr * cosine - vi * sine).astype(BF16)
                left[o, c, i, :, n:] = (vr * sine + vi * cosine).astype(BF16)
        return carry

    lax.fori_loop(0, nx * ny, rotate, 0)
    ready()
    lax.fori_loop(0, nx * ny, step, 0)


def meson_kernel(
    count, norm, disp_ref, v_ref, link_ref, phase_ref, per_hbm, elem_ref, corr_ref,
    pad, links, fields, left, part, got, own, rows_in, ring, mixed, sand, acc, per_ref, per_sem, v_sem, pair_send, pair_recv, send_sem, recv_sem,
):
    seps, spins, n, wide = per_ref.shape
    fetch = pltpu.make_async_copy(per_hbm, per_ref, per_sem)
    inner = pad.at[:, :, pl.ds(1, v_ref.shape[2])]
    fetch_v = pltpu.make_async_copy(v_ref, inner, v_sem)
    fetch_v.start()
    fetch.start()
    half = own.shape[0]
    mine_rows = elem_ref.shape[1]
    cfg, t, s = lax.axis_index("cfg"), lax.axis_index("tm"), lax.axis_index("space")
    other = 1 - s
    partner = (cfg, t, other)
    ringed = count == 8 and seps == 8
    if ringed:
        odd = t % 2
        place = (1 - odd) * (t // 2) + odd * ((15 - t) // 2)

        def at_place(p):
            p = (p + 16) % 8
            high = p // 4
            return (1 - high) * (2 * p) + high * (15 - 2 * p)

        targets = [at_place(place + 1), at_place(place - 1)]
        greet = list(targets)
    else:
        targets = [(t + d) % count for d in range(1, seps)]
        greet = targets + [(t + count - d) % count for d in range(1, seps)]

    barrier = pltpu.get_barrier_semaphore()
    pl.semaphore_signal(barrier, inc=1, device_id=partner, device_id_type=MESH)
    for g in greet:
        pl.semaphore_signal(barrier, inc=1, device_id=(cfg, g, s), device_id_type=MESH)
    pl.semaphore_wait(barrier, 1 + len(greet))

    def pair(src, dst, k):
        copy = pltpu.make_async_remote_copy(
            src_ref=src, dst_ref=dst, send_sem=pair_send.at[k], recv_sem=pair_recv.at[k],
            device_id=partner, device_id_type=MESH,
        )
        copy.start()
        return copy

    nx = v_ref.shape[2]
    rows = fields.shape[1] * fields.shape[2] * fields.shape[3]
    halo = [
        pair(v_ref.at[:, :, nx - 1], pad.at[:, :, 0], half + 2),
        pair(v_ref.at[:, :, 0], pad.at[:, :, nx + 1], half + 3),
        pair(link_ref.at[nx - 1], links.at[0], half + 4),
    ]
    links[1:] = link_ref[...]
    fetch_v.wait()

    def ready():
        for copy in halo:
            copy.wait_recv()

    make_fields(ready, v_ref, phase_ref, links, pad, fields, left)

    def project(o):
        lhs = left[o].reshape(rows, wide)
        rhs = fields[disp_ref[o]].reshape(rows, wide)
        block = lax.dot_general(lhs, rhs, (((0,), (0,)), ((), ())), preferred_element_type=F32)
        return combine(block, n)

    first = {}
    middle = half // 2
    order = [g + w * middle for g in range(middle) for w in range(2)]

    def project_other(o):
        part[o, :, :n], part[o, :, n:] = project(other * half + o)
        first[o] = pair(part.at[o], got.at[o], o)

    project_other(order[0])

    if ringed:
        pieces = half
        size = half // pieces

        def hop(way, k, g):
            span = pl.ds(g * size, size)
            src = own.at[span] if k == 0 else ring.at[way * 4 + k - 1, span]
            return pltpu.make_async_remote_copy(
                src_ref=src, dst_ref=ring.at[way * 4 + k, span],
                send_sem=send_sem.at[way, k, g], recv_sem=recv_sem.at[way, k, g],
                device_id=(cfg, targets[way], s), device_id_type=MESH,
            )

    hops = {}
    for at, o in enumerate(order):
        if at + 1 < half:
            project_other(order[at + 1])
        real, imag = project(s * half + o)
        first[o].wait_recv()
        own[o, :, :n] = ((real + got[o, :, :n]) * norm).astype(BF16)
        own[o, :, n:] = ((imag + got[o, :, n:]) * norm).astype(BF16)
        if ringed:
            way = o // middle
            hops[way, 0, o] = hop(way, 0, o)
            hops[way, 0, o].start()
    if ringed:
        for o in range(half):
            way = 1 - o // middle
            hops[way, 0, o] = hop(way, 0, o)
            hops[way, 0, o].start()
    if not ringed:
        for k in range(seps - 1):
            hops[k] = pltpu.make_async_remote_copy(
                src_ref=own, dst_ref=ring.at[k], send_sem=send_sem.at[k, 0, 0],
                recv_sem=recv_sem.at[k, 0, 0],
                device_id=(cfg, targets[k], s), device_id_type=MESH,
            )
            hops[k].start()
    rows_copy = pair(own.at[:, pl.ds(other * mine_rows, mine_rows)], rows_in, half)
    elem_ref[pl.ds(s * half, half)] = own[:, pl.ds(s * mine_rows, mine_rows)]

    def sandwich(d):
        flat = own[...].reshape(half * n, wide)
        for a in range(spins):
            spin = per_ref[d, a]
            turned = jnp.concatenate([-spin[:, n:], spin[:, :n]], axis=1)
            block = jnp.concatenate([spin, turned], axis=0)
            prod = jnp.dot(flat, block, preferred_element_type=F32).astype(BF16)
            for o in range(half):
                mixed[a * n : (a + 1) * n, o * wide : (o + 1) * wide] = prod[o * n : (o + 1) * n]
        lhs = per_ref[d].reshape(spins * n, wide).T
        for o in range(half):
            both = jnp.dot(lhs, mixed[:, o * wide : (o + 1) * wide], preferred_element_type=F32)
            real, imag = combine(both, n)
            sand[o, :, :n] = real
            sand[o, :, n:] = imag

    def contract(d, block):
        for o in range(half):
            term = jnp.sum(block[o].astype(F32) * sand[o], axis=0, keepdims=True)
            acc[s, d, pl.ds(o, 1)] = (term[:, :n] + term[:, n:]) * (1.0 / n)

    fetch.wait()
    sandwich(0)
    contract(0, own)
    if ringed:
        for k in range(1, 5):
            for j in range(pieces):
                for way in range(2):
                    g = (j + way * middle) % half
                    if (way, k - 1, g) not in hops or k == 4:
                        continue
                    hops[way, k - 1, g].wait_recv()
                    if k < 3 or g // middle == way:
                        hops[way, k, g] = hop(way, k, g)
                        hops[way, k, g].start()
            if k < 4:
                for way in range(2):
                    source = at_place(place - k if way == 0 else place + k)
                    d = (t - source + 8) % 8
                    sandwich(d)
                    contract(d, ring.at[way * 4 + k - 1])
            else:
                d = (t - at_place(place + 4) + 8) % 8
                sandwich(d)
                for o in range(half):
                    way = o // middle
                    hops[way, 3, o].wait_recv()
                    term = jnp.sum(ring[way * 4 + 3, o].astype(F32) * sand[o], axis=0, keepdims=True)
                    acc[s, d, pl.ds(o, 1)] = (term[:, :n] + term[:, n:]) * (1.0 / n)
    else:
        for k in range(seps - 1):
            sandwich(k + 1)
            hops[k].wait_recv()
            contract(k + 1, ring.at[k])
    last = pair(acc.at[s], acc.at[s], half + 1)
    rows_copy.wait_recv()
    elem_ref[pl.ds(other * half, half)] = rows_in[...]
    for copy in hops.values():
        copy.wait_send()
    for copy in halo + list(first.values()):
        copy.wait_send()
    rows_copy.wait_send()
    last.wait()
    corr_ref[...] = acc[...]


def body(vectors, gauge_links, perambulators, momenta, displacements):
    space_index = lax.axis_index("space")
    space_count = lax.axis_size("space")
    count = lax.axis_size("tm")
    field = vectors[0]
    _, _, nx, ny, nz, n = field.shape
    ops = momenta.shape[0]
    links = gauge_links[0]
    links = jnp.transpose(links.reshape(54, nx, ny, nz), (1, 2, 3, 0))

    extent_x = nx * space_count
    xs = (space_index * nx + jnp.arange(nx, dtype=jnp.int32)).astype(F32)
    ys = jnp.arange(ny, dtype=jnp.int32).astype(F32)
    zs = jnp.arange(nz, dtype=jnp.int32).astype(F32)
    mom = momenta.astype(F32)
    angle = (mom[:, 0] * xs[:, None] / extent_x)[:, None, None, :]
    angle = angle + (mom[:, 1] * ys[:, None] / ny)[None, :, None, :]
    angle = angle + (mom[:, 2] * zs[:, None] / nz)[None, None, :, :]
    angle = 2.0 * math.pi * angle
    phases = jnp.concatenate([jnp.cos(angle), jnp.sin(angle)], axis=-1)

    vmem = pl.BlockSpec(memory_space=pltpu.VMEM)
    hbm = pl.BlockSpec(memory_space=pltpu.HBM)
    perams = perambulators[0]
    seps, spins = perams.shape[:2]
    half = ops // 2
    norm = 1.0 / math.sqrt(6.0 * extent_x * ny * nz)
    elementals, corr = pl.pallas_call(
        functools.partial(meson_kernel, count, norm),
        out_shape=(
            jax.ShapeDtypeStruct((ops, n // 2, 2 * n), BF16),
            jax.ShapeDtypeStruct((2, seps, half, n), F32),
        ),
        in_specs=[pl.BlockSpec(memory_space=pltpu.SMEM), hbm, vmem, vmem, hbm],
        out_specs=(vmem, vmem),
        scratch_shapes=[
            pltpu.VMEM((2, 3, nx + 2, ny, nz, n), BF16),
            pltpu.VMEM((nx + 1, ny, nz, 54), F32),
            pltpu.VMEM((4, 3, nx * ny, nz, 2 * n), BF16),
            pltpu.VMEM((ops, 3, nx * ny, nz, 2 * n), BF16),
            pltpu.VMEM((half, n, 2 * n), F32),
            pltpu.VMEM((half, n, 2 * n), F32),
            pltpu.VMEM((half, n, 2 * n), BF16),
            pltpu.VMEM((half, n // 2, 2 * n), BF16),
            pltpu.VMEM((8, half, n, 2 * n), BF16),
            pltpu.VMEM((spins * n, half * 2 * n), BF16),
            pltpu.VMEM((half, n, 2 * n), F32),
            pltpu.VMEM((2, seps, half, n), F32),
            pltpu.VMEM(perams.shape, BF16),
            pltpu.SemaphoreType.DMA,
            pltpu.SemaphoreType.DMA,
            pltpu.SemaphoreType.DMA((half + 5,)),
            pltpu.SemaphoreType.DMA((half + 5,)),
            pltpu.SemaphoreType.DMA((8, 4, half)),
            pltpu.SemaphoreType.DMA((8, 4, half)),
        ],
        compiler_params=pltpu.CompilerParams(
            collective_id=0, has_side_effects=True, vmem_limit_bytes=48 * 2**20
        ),
        name="mesons",
    )(displacements, field, links, phases, perams)
    corr = jnp.sum(corr, axis=-1)
    corr = jnp.transpose(corr, (0, 2, 1)).reshape(ops, 1, seps)
    return (elementals[None], corr)


def solution(mesh):
    return jax.shard_map(
        body,
        mesh=mesh,
        in_specs=(
            P(("cfg", "tm"), None, None, "space", None, None, None),
            P(("cfg", "tm"), None, None, None, None, "space", None, None),
            P(("cfg", "tm"), None, None, None, None),
            P(),
            P(),
        ),
        out_specs=(P(("cfg", "tm"), None, "space", None), P(None, ("cfg", "tm"), None)),
        check_vma=False,
    )
```

```python
import functools
import math

import jax
import jax.numpy as jnp
from jax import lax
from jax.experimental import pallas as pl
from jax.experimental.pallas import tpu as pltpu
from jax.sharding import PartitionSpec as P

F32 = jnp.float32
BF16 = jnp.bfloat16
MESH = pl.DeviceIdType.MESH


def combine(block, n):
    real = block[:n, :n] + block[n:, n:]
    imag = block[:n, n:] - block[n:, :n]
    return real, imag


def make_fields(ready, v_ref, phase_ref, links_ref, pad, fields, left):
    _, _, nx, ny, nz, n = v_ref.shape
    ops = left.shape[0]

    def spread(table, column):
        return jnp.broadcast_to(table[:, column : column + 1], (nz, n))

    def load(x, y):
        return [[pad[r, c, x, y].astype(F32) for c in range(3)] for r in range(2)]

    def times(link, field, adjoint):
        real, imag = [], []
        for t in range(3):
            re, im = None, None
            for s in range(3):
                at = s * 3 + t if adjoint else t * 3 + s
                er, ei = link[at], link[9 + at]
                fr, fi = field[0][s], field[1][s]
                if adjoint:
                    a, b = er * fr + ei * fi, er * fi - ei * fr
                else:
                    a, b = er * fr - ei * fi, er * fi + ei * fr
                re = a if re is None else re + a
                im = b if im is None else im + b
            real.append(re)
            imag.append(im)
        return [real, imag]

    def rolled(field, shift):
        return [[pltpu.roll(e, shift, axis=0) for e in part] for part in field]

    def step(i, carry):
        x, y = i // ny, i % ny
        here = load(x + 1, y)
        table = links_ref[x + 1, y]
        back_x = links_ref[x, y]
        y_down = (y + ny - 1) % ny
        back_y = links_ref[x + 1, y_down]
        total = None

        def add(total, field):
            if total is None:
                return field
            return [[a + b for a, b in zip(p, q)] for p, q in zip(total, field)]

        for mu in range(3):
            link = [spread(table, mu * 18 + e) for e in range(18)]
            if mu == 0:
                ahead = load(x + 2, y)
            elif mu == 1:
                ahead = load(x + 1, (y + 1) % ny)
            else:
                ahead = rolled(here, nz - 1)
            forward = times(link, ahead, False)
            total = add(total, forward)
            for r in range(2):
                for c in range(3):
                    fields[mu + 1, c, i, :, r * n : (r + 1) * n] = forward[r][c].astype(BF16)
            if mu == 0:
                behind = [spread(back_x, e) for e in range(18)]
                backward = times(behind, load(x, y), True)
            elif mu == 1:
                behind = [spread(back_y, 18 + e) for e in range(18)]
                backward = times(behind, load(x + 1, y_down), True)
            else:
                backward = rolled(times(link, here, True), 1)
            total = add(total, backward)
        for r in range(2):
            for c in range(3):
                smooth = here[r][c] - total[r][c] / 6.0
                fields[0, c, i, :, r * n : (r + 1) * n] = smooth.astype(BF16)
        return carry

    def rotate(i, carry):
        x, y = i // ny, i % ny
        angles = phase_ref[x, y]
        for o in range(ops):
            cosine = spread(angles, o)
            sine = spread(angles, ops + o)
            for c in range(3):
                vr, vi = pad[0, c, x + 1, y].astype(F32), pad[1, c, x + 1, y].astype(F32)
                left[o, c, i, :, :n] = (vr * cosine - vi * sine).astype(BF16)
                left[o, c, i, :, n:] = (vr * sine + vi * cosine).astype(BF16)
        return carry

    lax.fori_loop(0, nx * ny, rotate, 0)
    ready()
    lax.fori_loop(0, nx * ny, step, 0)


def meson_kernel(
    count, norm, disp_ref, v_ref, link_ref, phase_ref, per_hbm, elem_ref, corr_ref,
    pad, links, fields, left, part, got, own, rows_in, ring, mixed, sand, acc, per_ref, per_sem, v_sem, pair_send, pair_recv, send_sem, recv_sem,
):
    seps, spins, n, wide = per_ref.shape
    fetch = pltpu.make_async_copy(per_hbm, per_ref, per_sem)
    inner = pad.at[:, :, pl.ds(1, v_ref.shape[2])]
    fetch_v = pltpu.make_async_copy(v_ref, inner, v_sem)
    fetch_v.start()
    fetch.start()
    half = own.shape[0]
    mine_rows = elem_ref.shape[1]
    cfg, t, s = lax.axis_index("cfg"), lax.axis_index("tm"), lax.axis_index("space")
    other = 1 - s
    partner = (cfg, t, other)
    ringed = count == 8 and seps == 8
    if ringed:
        odd = t % 2
        place = (1 - odd) * (t // 2) + odd * ((15 - t) // 2)

        def at_place(p):
            p = (p + 16) % 8
            high = p // 4
            return (1 - high) * (2 * p) + high * (15 - 2 * p)

        targets = [at_place(place + 1), at_place(place - 1)]
        greet = list(targets)
    else:
        targets = [(t + d) % count for d in range(1, seps)]
        greet = targets + [(t + count - d) % count for d in range(1, seps)]

    barrier = pltpu.get_barrier_semaphore()
    pl.semaphore_signal(barrier, inc=1, device_id=partner, device_id_type=MESH)
    for g in greet:
        pl.semaphore_signal(barrier, inc=1, device_id=(cfg, g, s), device_id_type=MESH)
    pl.semaphore_wait(barrier, 1 + len(greet))

    def pair(src, dst, k):
        copy = pltpu.make_async_remote_copy(
            src_ref=src, dst_ref=dst, send_sem=pair_send.at[k], recv_sem=pair_recv.at[k],
            device_id=partner, device_id_type=MESH,
        )
        copy.start()
        return copy

    nx = v_ref.shape[2]
    rows = fields.shape[1] * fields.shape[2] * fields.shape[3]
    halo = [
        pair(v_ref.at[:, :, nx - 1], pad.at[:, :, 0], half + 2),
        pair(v_ref.at[:, :, 0], pad.at[:, :, nx + 1], half + 3),
        pair(link_ref.at[nx - 1], links.at[0], half + 4),
    ]
    links[1:] = link_ref[...]
    fetch_v.wait()

    def ready():
        for copy in halo:
            copy.wait_recv()

    make_fields(ready, v_ref, phase_ref, links, pad, fields, left)

    def project(o):
        lhs = left[o].reshape(rows, wide)
        rhs = fields[disp_ref[o]].reshape(rows, wide)
        block = lax.dot_general(lhs, rhs, (((0,), (0,)), ((), ())), preferred_element_type=F32)
        return combine(block, n)

    first = {}
    middle = half // 2
    order = [g + w * middle for g in range(middle) for w in range(2)]

    def project_other(o):
        part[o, :, :n], part[o, :, n:] = project(other * half + o)
        first[o] = pair(part.at[o], got.at[o], o)

    project_other(order[0])

    if ringed:
        pieces = half
        size = half // pieces

        def hop(way, k, g):
            span = pl.ds(g * size, size)
            src = own.at[span] if k == 0 else ring.at[way * 4 + k - 1, span]
            return pltpu.make_async_remote_copy(
                src_ref=src, dst_ref=ring.at[way * 4 + k, span],
                send_sem=send_sem.at[way, k, g], recv_sem=recv_sem.at[way, k, g],
                device_id=(cfg, targets[way], s), device_id_type=MESH,
            )

    hops = {}
    for at, o in enumerate(order):
        if at + 1 < half:
            project_other(order[at + 1])
        real, imag = project(s * half + o)
        first[o].wait_recv()
        own[o, :, :n] = ((real + got[o, :, :n]) * norm).astype(BF16)
        own[o, :, n:] = ((imag + got[o, :, n:]) * norm).astype(BF16)
        if ringed:
            way = o // middle
            hops[way, 0, o] = hop(way, 0, o)
            hops[way, 0, o].start()
    if ringed:
        for o in range(half):
            way = 1 - o // middle
            hops[way, 0, o] = hop(way, 0, o)
            hops[way, 0, o].start()
    if not ringed:
        for k in range(seps - 1):
            hops[k] = pltpu.make_async_remote_copy(
                src_ref=own, dst_ref=ring.at[k], send_sem=send_sem.at[k, 0, 0],
                recv_sem=recv_sem.at[k, 0, 0],
                device_id=(cfg, targets[k], s), device_id_type=MESH,
            )
            hops[k].start()
    rows_copy = pair(own.at[:, pl.ds(other * mine_rows, mine_rows)], rows_in, half)
    elem_ref[pl.ds(s * half, half)] = own[:, pl.ds(s * mine_rows, mine_rows)]

    def sandwich(d):
        flat = own[...].reshape(half * n, wide)
        for a in range(spins):
            spin = per_ref[d, a]
            turned = jnp.concatenate([-spin[:, n:], spin[:, :n]], axis=1)
            block = jnp.concatenate([spin, turned], axis=0)
            prod = jnp.dot(flat, block, preferred_element_type=F32).astype(BF16)
            for o in range(half):
                mixed[a * n : (a + 1) * n, o * wide : (o + 1) * wide] = prod[o * n : (o + 1) * n]
        lhs = per_ref[d].reshape(spins * n, wide).T
        for o in range(half):
            both = jnp.dot(lhs, mixed[:, o * wide : (o + 1) * wide], preferred_element_type=F32)
            real, imag = combine(both, n)
            sand[o, :, :n] = real
            sand[o, :, n:] = imag

    def contract(d, block):
        for o in range(half):
            term = jnp.sum(block[o].astype(F32) * sand[o], axis=0, keepdims=True)
            acc[s, o, pl.ds(d, 1)] = (term[:, :n] + term[:, n:]) * (1.0 / n)

    fetch.wait()
    sandwich(0)
    contract(0, own)
    if ringed:
        for k in range(1, 5):
            for j in range(pieces):
                for way in range(2):
                    g = (j + way * middle) % half
                    if (way, k - 1, g) not in hops or k == 4:
                        continue
                    hops[way, k - 1, g].wait_recv()
                    if k < 3 or g // middle == way:
                        hops[way, k, g] = hop(way, k, g)
                        hops[way, k, g].start()
            if k < 4:
                for way in range(2):
                    source = at_place(place - k if way == 0 else place + k)
                    d = (t - source + 8) % 8
                    sandwich(d)
                    contract(d, ring.at[way * 4 + k - 1])
            else:
                d = (t - at_place(place + 4) + 8) % 8
                sandwich(d)
                for o in range(half):
                    way = o // middle
                    hops[way, 3, o].wait_recv()
                    term = jnp.sum(ring[way * 4 + 3, o].astype(F32) * sand[o], axis=0, keepdims=True)
                    acc[s, o, pl.ds(d, 1)] = (term[:, :n] + term[:, n:]) * (1.0 / n)
    else:
        for k in range(seps - 1):
            sandwich(k + 1)
            hops[k].wait_recv()
            contract(k + 1, ring.at[k])
    last = pair(acc.at[s], acc.at[s], half + 1)
    rows_copy.wait_recv()
    elem_ref[pl.ds(other * half, half)] = rows_in[...]
    for copy in hops.values():
        copy.wait_send()
    for copy in halo + list(first.values()):
        copy.wait_send()
    rows_copy.wait_send()
    last.wait()
    corr_ref[...] = acc[...]


def body(vectors, gauge_links, perambulators, momenta, displacements):
    space_index = lax.axis_index("space")
    space_count = lax.axis_size("space")
    count = lax.axis_size("tm")
    field = vectors[0]
    _, _, nx, ny, nz, n = field.shape
    ops = momenta.shape[0]
    links = gauge_links[0]
    links = jnp.transpose(links.reshape(54, nx, ny, nz), (1, 2, 3, 0))

    extent_x = nx * space_count
    xs = (space_index * nx + jnp.arange(nx, dtype=jnp.int32)).astype(F32)
    ys = jnp.arange(ny, dtype=jnp.int32).astype(F32)
    zs = jnp.arange(nz, dtype=jnp.int32).astype(F32)
    mom = momenta.astype(F32)
    angle = (mom[:, 0] * xs[:, None] / extent_x)[:, None, None, :]
    angle = angle + (mom[:, 1] * ys[:, None] / ny)[None, :, None, :]
    angle = angle + (mom[:, 2] * zs[:, None] / nz)[None, None, :, :]
    angle = 2.0 * math.pi * angle
    phases = jnp.concatenate([jnp.cos(angle), jnp.sin(angle)], axis=-1)

    vmem = pl.BlockSpec(memory_space=pltpu.VMEM)
    hbm = pl.BlockSpec(memory_space=pltpu.HBM)
    perams = perambulators[0]
    seps, spins = perams.shape[:2]
    half = ops // 2
    norm = 1.0 / math.sqrt(6.0 * extent_x * ny * nz)
    elementals, corr = pl.pallas_call(
        functools.partial(meson_kernel, count, norm),
        out_shape=(
            jax.ShapeDtypeStruct((ops, n // 2, 2 * n), BF16),
            jax.ShapeDtypeStruct((2, half, seps, n), F32),
        ),
        in_specs=[pl.BlockSpec(memory_space=pltpu.SMEM), hbm, vmem, vmem, hbm],
        out_specs=(vmem, vmem),
        scratch_shapes=[
            pltpu.VMEM((2, 3, nx + 2, ny, nz, n), BF16),
            pltpu.VMEM((nx + 1, ny, nz, 54), F32),
            pltpu.VMEM((4, 3, nx * ny, nz, 2 * n), BF16),
            pltpu.VMEM((ops, 3, nx * ny, nz, 2 * n), BF16),
            pltpu.VMEM((half, n, 2 * n), F32),
            pltpu.VMEM((half, n, 2 * n), F32),
            pltpu.VMEM((half, n, 2 * n), BF16),
            pltpu.VMEM((half, n // 2, 2 * n), BF16),
            pltpu.VMEM((8, half, n, 2 * n), BF16),
            pltpu.VMEM((spins * n, half * 2 * n), BF16),
            pltpu.VMEM((half, n, 2 * n), F32),
            pltpu.VMEM((2, half, seps, n), F32),
            pltpu.VMEM(perams.shape, BF16),
            pltpu.SemaphoreType.DMA,
            pltpu.SemaphoreType.DMA,
            pltpu.SemaphoreType.DMA((half + 5,)),
            pltpu.SemaphoreType.DMA((half + 5,)),
            pltpu.SemaphoreType.DMA((8, 4, half)),
            pltpu.SemaphoreType.DMA((8, 4, half)),
        ],
        compiler_params=pltpu.CompilerParams(
            collective_id=0, has_side_effects=True, vmem_limit_bytes=48 * 2**20
        ),
        name="mesons",
    )(displacements, field, links, phases, perams)
    corr = jnp.sum(corr, axis=-1).reshape(ops, 1, seps)
    return (elementals[None], corr)


def solution(mesh):
    return jax.shard_map(
        body,
        mesh=mesh,
        in_specs=(
            P(("cfg", "tm"), None, None, "space", None, None, None),
            P(("cfg", "tm"), None, None, None, None, "space", None, None),
            P(("cfg", "tm"), None, None, None, None),
            P(),
            P(),
        ),
        out_specs=(P(("cfg", "tm"), None, "space", None), P(None, ("cfg", "tm"), None)),
        check_vma=False,
    )
```
